32 devices in a mesh: rep: 4 (over y, x), fsdp: 8 (over z, core).
Axes of the slice: x: 2, y: 2, z: 4, core: 2. Of those that a mesh axis runs over, the one named last changes fastest.
Arguments:
- activations: bfloat16 [8192, 512], P(('rep', 'fsdp')), may hold values from -6 to 6
- output_grads: bfloat16 [8192, 8192], P(('rep', 'fsdp'))
- master: float32 [8192, 512], P('fsdp'), may hold values from -6 to 6
- first_moment: float32 [8192, 512], P('fsdp'), may hold values from -4 to 4
- second_moment: float32 [8192, 512], P('fsdp'), may hold values from 0.2 to 2
Outputs:
- new_master: float32 [8192, 512], P('fsdp')
- new_first: float32 [8192, 512], P('fsdp')
- new_second: float32 [8192, 512], P('fsdp')
- params: bfloat16 [8192, 512], replicated
The draws below stay inside these ranges and needn't reach their ends.
All inputs are finite; a program needn't handle non-finite values.
Results may differ from the reference program's by a relative error of at most 0.0004.
Values may be sent and summed in bfloat16 or wider, within the bound.
A program may use at most 128 MiB of HBM per device.

```python
import math
import jax
import jax.numpy as jnp
from jax import lax

D = 8192
ROWS = 512
TOK_DEV = 256
LEVELS = 2
TOKENS = 2048
BATCH = 8192
N_REP = 4
N_FSDP = 8


def draw_activations(key, part):
    key_common, key_own = jax.random.split(jax.random.fold_in(key, 11))
    common = jax.random.normal(key_common, (TOKENS, ROWS), jnp.float32)
    own_part = jax.random.normal(key_own, (N_REP, TOKENS, ROWS), jnp.float32)
    share = 0.8
    mixed = share * common[None] + math.sqrt(1.0 - share * share) * own_part
    mixed = jnp.clip(mixed, -6.0, 6.0)
    return mixed.reshape(BATCH, ROWS).astype(jnp.bfloat16)


def draw_output_grads(key, part):
    key_common, key_own, key_gain, key_block = jax.random.split(jax.random.fold_in(key, 23), 4)
    common = jax.random.normal(key_common, (TOKENS, D), jnp.float32)
    own_part = jax.random.normal(key_own, (N_REP, TOKENS, D), jnp.float32)
    share = 0.7
    mixed = jnp.clip(share * common[None] + math.sqrt(1.0 - share * share) * own_part, -6.0, 6.0)
    device_place = (jnp.arange(TOKENS) // TOK_DEV).astype(jnp.float32)
    rising = 1.0 + 2.0 * device_place / max(N_FSDP - 1, 1)
    gains = jax.random.uniform(key_gain, (N_REP,), jnp.float32, 0.5, 2.0)
    block_count = N_FSDP * N_REP
    block_width = D // block_count
    block_logs = jax.random.uniform(key_block, (N_REP, block_count), jnp.float32, -0.8, 0.8)
    block_scale = jnp.repeat(jnp.exp(block_logs), block_width, axis=1)
    scaled = mixed * rising[None, :, None] * gains[:, None, None] * block_scale[:, None, :] / math.sqrt(TOKENS)
    return scaled.reshape(BATCH, D).astype(jnp.bfloat16)


def levels(stream_key, dims, cuts, low, largest):
    factor_of = 1.0
    for axis_at, blocks in cuts:
        heights = jax.random.uniform(jax.random.fold_in(jax.random.fold_in(stream_key, 6), axis_at), (blocks,), jnp.float32, low / len(cuts), largest / len(cuts))
        factor_of = factor_of * jnp.repeat(jnp.exp(heights), dims[axis_at] // blocks).reshape((-1,) + (1,) * (len(dims) - 1 - axis_at))
    return factor_of


def gaussian(rng, dims, deviation, bound, cuts=(), kind=jnp.bfloat16):
    level = levels(rng, dims, cuts, -0.22, 0.18) if cuts else 1.0
    array = jax.random.normal(rng, dims, jnp.float32) * deviation * level
    return jnp.minimum(jnp.maximum(array, -bound), bound).astype(kind)


def setup_inputs(seed: int = 0) -> dict:
    arg_keys = jax.random.split(jax.random.key(seed), 6)
    return {
        "activations": draw_activations(jax.random.fold_in(arg_keys[5], 71), 0),
        "output_grads": draw_output_grads(jax.random.fold_in(arg_keys[5], 71), 0),
        "master": gaussian(arg_keys[2], (D, ROWS), 0.5, 6.0, ((0, 8),), jnp.float32),
        "first_moment": gaussian(arg_keys[3], (D, ROWS), 0.3, 4.0, ((0, 8),), jnp.float32),
        "second_moment": jnp.clip(jnp.exp(math.log(2.0) - 2.3025851 * jax.random.uniform(arg_keys[4], (D, ROWS), jnp.float32) ** levels(arg_keys[4], (D, ROWS), ((0, 8),), -0.2, 0.2)), 0.2, 2.0),
    }


dot_epsilon = 1e-06
beta_one = 0.9
beta_two = 0.95
adam_epsilon = 1e-08
learn_rate = 0.02
decay_rate = 0.1
contract_first = (((0,), (0,)), ((), ()))

def adasum_pair(left_vec, right_vec):
    cross = jnp.sum(left_vec * right_vec)
    left_sq = jnp.sum(left_vec * left_vec)
    right_sq = jnp.sum(right_vec * right_vec)
    return (1.0 - cross / (2.0 * (left_sq + dot_epsilon))) * left_vec + (1.0 - cross / (2.0 * (right_sq + dot_epsilon))) * right_vec

def reference(activations, output_grads, master, first_moment, second_moment):
    group_acts = activations.reshape(N_REP, TOKENS, ROWS)
    group_outs = output_grads.reshape(N_REP, TOKENS, D)
    vectors = []
    for replica in range(N_REP):
        vectors.append(lax.dot_general(group_outs[replica], group_acts[replica], contract_first, preferred_element_type=jnp.float32))
    for level_index in range(LEVELS):
        vectors = [adasum_pair(vectors[2 * pair_index], vectors[2 * pair_index + 1]) for pair_index in range(len(vectors) // 2)]
    combined = vectors[0]
    correct_one = 1.0 - (beta_one ** 50) ** 2
    correct_two = 1.0 - (beta_two ** 50) ** 2
    new_first = beta_one * first_moment + (1.0 - beta_one) * combined
    new_second = beta_two * second_moment + (1.0 - beta_two) * combined * combined
    update = new_first / correct_one / (jnp.sqrt(new_second / correct_two) + adam_epsilon) + decay_rate * master
    new_master = master - learn_rate * update
    return (new_master, new_first, new_second, new_master.astype(jnp.bfloat16))
```

```python
import functools

import jax
import jax.numpy as jnp
from jax import lax
from jax.experimental import pallas as pl
from jax.experimental.pallas import tpu as pltpu
from jax.sharding import PartitionSpec as P

dot_epsilon = 1e-06
beta_one = 0.9
beta_two = 0.95
adam_epsilon = 1e-08
learn_rate = 0.02
decay_rate = 0.1
correct_one = 1.0 - (beta_one**50) ** 2
correct_two = 1.0 - (beta_two**50) ** 2
contract_first = (((0,), (0,)), ((), ()))
MESH = pl.DeviceIdType.MESH


def drain(ref, sem):
    pltpu.make_async_copy(ref, ref, sem).wait()


def gram_pairs(count):
    return [(i, j) for i in range(count) for j in range(i, count)]


def adasum_coefs(gram, count):
    coefs = [None] * count
    members = [[i] for i in range(count)]
    scale = [1.0] * count

    def inner(left, right):
        total = 0.0
        for i in left:
            for j in right:
                total = total + scale[i] * scale[j] * gram[min(i, j), max(i, j)]
        return total

    while len(members) > 1:
        merged = []
        for left, right in zip(members[::2], members[1::2]):
            cross = inner(left, right)
            left_sq = jnp.maximum(inner(left, left), 0.0)
            right_sq = jnp.maximum(inner(right, right), 0.0)
            left_coef = 1.0 - cross / (2.0 * (left_sq + dot_epsilon))
            right_coef = 1.0 - cross / (2.0 * (right_sq + dot_epsilon))
            for i in left:
                scale[i] = left_coef * scale[i]
            for i in right:
                scale[i] = right_coef * scale[i]
            merged.append(left + right)
        members = merged
    for i in range(count):
        coefs[i] = scale[i]
    return coefs


def kernel(
    reps,
    n,
    act,
    og,
    master_in,
    first_in,
    second_in,
    master_out,
    first_out,
    second_out,
    params,
    y_all,
    x_all,
    grad,
    pieces,
    comb,
    state,
    rounded,
    dots_own,
    dots_rep,
    dots_sum,
    dots_fsdp,
    local_sem,
    own_sem,
    x_send,
    x_chain,
    x_recv,
    y_send,
    y_recv,
    p_send,
    p_recv,
    d_send,
    d_recv,
    c_send,
    c_recv,
    z_send,
    z_recv,
    w_send,
    w_recv,
    f_send,
    f_recv,
    s_send,
    s_recv,
):
    r = lax.axis_index("rep")
    f = lax.axis_index("fsdp")
    core = lax.rem(f, 2)
    chip = lax.div(f, 2)
    chips = n // 2
    sibling = chip * 2 + 1 - core
    tokens = act.shape[0]
    block = master_in.shape[0]
    piece = block // reps
    chunks, width = y_all.shape[0], y_all.shape[2]
    per_chunk = reps // chunks

    def remote(src, dst, send, recv, rep_to, fsdp_to):
        pltpu.make_async_remote_copy(
            src_ref=src,
            dst_ref=dst,
            send_sem=send,
            recv_sem=recv,
            device_id={"rep": rep_to, "fsdp": fsdp_to},
            device_id_type=MESH,
        ).start()

    def rows(start, size):
        return pl.ds(pl.multiple_of(start, 16), size)

    def chip_ahead(step):
        return lax.rem(chip + step, chips) * 2 + core

    def chip_behind(step):
        return lax.rem(chip - step + chips, chips) * 2 + core

    state_loads = [
        pltpu.make_async_copy(src, state.at[i], local_sem.at[i])
        for i, src in enumerate((master_in, first_in, second_in))
    ]
    for load in state_loads:
        load.start()
    own_x = pltpu.make_async_copy(act, x_all.at[rows(f * tokens, tokens)], local_sem.at[3])
    own_x.start()

    def own_y(s):
        column = pl.multiple_of(f * block + s * width, 128)
        return pltpu.make_async_copy(
            og.at[:, pl.ds(column, width)],
            y_all.at[s, rows(f * tokens, tokens)],
            own_sem.at[s],
        )

    for s in range(chunks):
        own_y(s).start()

    barrier = pltpu.get_barrier_semaphore()

    def greet_fsdp(step, carry):
        pl.semaphore_signal(
            barrier, inc=1, device_id={"rep": r, "fsdp": lax.rem(f + step, n)}, device_id_type=MESH
        )
        return carry

    lax.fori_loop(1, n, greet_fsdp, 0)

    def greet_rep(step, carry):
        pl.semaphore_signal(
            barrier, inc=1, device_id={"rep": lax.rem(r + step, reps), "fsdp": f}, device_id_type=MESH
        )
        return carry

    lax.fori_loop(1, reps, greet_rep, 0)
    pl.semaphore_wait(barrier, n + reps - 2)

    def x_slot(at_chip):
        return x_all.at[rows((at_chip * 2 + core) * tokens, tokens)]

    def send_x(src, slot, way, step):
        @pl.when((chip + 1 < chips) if way == 0 else (chip > 0))
        def _():
            to = (chip + 1 - 2 * way) * 2 + core
            remote(src, slot, x_send.at[way], x_chain.at[way, step], r, to)

    for way in range(2):
        send_x(act, x_slot(chip), way, 0)
    remote(act, x_slot(chip), x_send.at[2], x_recv, r, sibling)

    def place_of(s):
        return lax.rem(r + 1 + s, chunks)

    def send_y(index, carry):
        s = place_of(index // (n - 1))
        to = lax.rem(f + 1 + index % (n - 1), n)
        column = pl.multiple_of(to * block + s * width, 128)
        remote(
            og.at[:, pl.ds(column, width)],
            y_all.at[s, rows(f * tokens, tokens)],
            y_send.at[s],
            y_recv.at[s],
            r,
            to,
        )
        return carry

    early = (chunks + 1) // 2 * (n - 1)
    lax.fori_loop(0, early, send_y, 0)

    def relay_x(step, carry):
        for way in range(2):
            origin = chip - step * (1 - 2 * way)

            @pl.when((origin >= 0) if way == 0 else (origin < chips))
            def _():
                slot = x_slot(origin)
                drain(slot, x_chain.at[way, step - 1])
                send_x(slot, slot, way, step)
                remote(slot, slot, x_send.at[2], x_recv, r, sibling)

        return carry

    lax.fori_loop(1, chips, relay_x, 0)
    lax.fori_loop(early, chunks * (n - 1), send_y, 0)
    own_x.wait()
    drain(x_all.at[pl.ds(0, chips * tokens)], x_recv)

    depth = min(n * tokens, 2048)

    def chunk_sum(at_chunk, carry):
        s = place_of(at_chunk)
        own_y(s).wait()
        drain(y_all.at[s, pl.ds(0, (n - 1) * tokens)], y_recv.at[s])
        target = rows(s * width, width)
        grad[target, :] = lax.dot_general(
            y_all[s, pl.ds(0, depth), :],
            x_all[pl.ds(0, depth), :],
            contract_first,
            preferred_element_type=jnp.float32,
        )

        def more(at, inner):
            span = rows(at * depth, depth)
            grad[target, :] += lax.dot_general(
                y_all[s, span, :],
                x_all[span, :],
                contract_first,
                preferred_element_type=jnp.float32,
            )
            return inner

        lax.fori_loop(1, n * tokens // depth, more, 0)
        for sub in range(per_chunk):
            j = s * per_chunk + sub

            @pl.when(j != r)
            def _():
                remote(
                    grad.at[rows(j * piece, piece)], pieces.at[r], p_send, p_recv, j, f
                )

        return carry

    lax.fori_loop(0, chunks, chunk_sum, 0)
    pieces[r] = grad[rows(r * piece, piece), :]
    drain(pieces.at[pl.ds(0, reps - 1)], p_recv)

    pairs = gram_pairs(reps)
    lanes = 128

    def slab_dots(at, sums):
        span = pl.ds(pl.multiple_of(at * 8, 8), 8)
        parts = [pieces[i, span, :] for i in range(reps)]
        return tuple(total + parts[i] * parts[j] for total, (i, j) in zip(sums, pairs))

    zero = jnp.zeros((8, pieces.shape[2]), jnp.float32)
    sums = lax.fori_loop(0, piece // 8, slab_dots, (zero,) * len(pairs))
    dots_own[...] = jnp.zeros_like(dots_own)
    for at, total in enumerate(sums):
        line = jnp.sum(total, axis=0, keepdims=True)
        folded = line[:, 0:lanes]
        for start in range(lanes, line.shape[1], lanes):
            folded = folded + line[:, start : start + lanes]
        dots_own[at : at + 1, :] = folded

    def send_dots_rep(step, carry):
        remote(dots_own, dots_rep.at[r], d_send.at[0], d_recv.at[0], lax.rem(r + step, reps), f)
        return carry

    lax.fori_loop(1, reps, send_dots_rep, 0)
    dots_rep[r] = dots_own[...]
    drain(dots_rep.at[pl.ds(0, reps - 1)], d_recv.at[0])
    dots_sum[...] = jnp.sum(dots_rep[...], axis=0)

    def send_dots_fsdp(step, carry):
        remote(dots_sum, dots_fsdp.at[f], d_send.at[1], d_recv.at[1], r, lax.rem(f + step, n))
        return carry

    lax.fori_loop(1, n, send_dots_fsdp, 0)
    dots_fsdp[f] = dots_sum[...]
    drain(dots_fsdp.at[pl.ds(0, n - 1)], d_recv.at[1])
    dots_all = jnp.sum(jnp.sum(dots_fsdp[...], axis=0), axis=1, keepdims=True)
    features = pieces.shape[2]
    gram = {
        pair: jnp.broadcast_to(dots_all[at : at + 1, :], (1, features))
        for at, pair in enumerate(pairs)
    }
    coefs = adasum_coefs(gram, reps)

    own_rows = rows(r * piece, piece)
    for load in state_loads:
        load.wait()

    slab = 16

    def step_rows(start, combined):
        span = rows(start, slab)
        new_first = beta_one * state[1, span, :] + (1.0 - beta_one) * combined
        new_second = beta_two * state[2, span, :] + (1.0 - beta_two) * combined * combined
        update = (
            new_first / correct_one / (jnp.sqrt(new_second / correct_two) + adam_epsilon)
            + decay_rate * state[0, span, :]
        )
        new_master = state[0, span, :] - learn_rate * update
        state[0, span, :] = new_master
        state[1, span, :] = new_first
        state[2, span, :] = new_second
        rounded[span, :] = new_master.astype(jnp.bfloat16)

    def own_step(at, carry):
        span = rows(at * slab, slab)
        combined = coefs[0] * pieces[0, span, :]
        for i in range(1, reps):
            combined = combined + coefs[i] * pieces[i, span, :]
        comb[rows(r * piece + at * slab, slab), :] = combined
        return carry

    lax.fori_loop(0, piece // slab, own_step, 0)

    across = reps - 1 - r
    across_rows = rows(across * piece, piece)

    def other_reps(fn, carry):
        def body(step, inner):
            j = lax.rem(r + step, reps)

            @pl.when(j != across)
            def _():
                fn(j)

            return inner

        return lax.fori_loop(1, reps, body, carry)

    remote(comb.at[own_rows], comb.at[own_rows], c_send, c_recv.at[0], across, f)
    other_reps(
        lambda j: remote(comb.at[own_rows], comb.at[own_rows], c_send, c_recv.at[1], j, f), 0
    )

    def adam_piece(j):
        def body(at, carry):
            start = j * piece + at * slab
            step_rows(start, comb[rows(start, slab), :])
            return carry

        lax.fori_loop(0, piece // slab, body, 0)

    def send_piece(j, span, send, recv):
        def body(step, carry):
            remote(
                rounded.at[span],
                params.at[rows(f * block + j * piece, piece)],
                send,
                recv.at[step],
                r,
                chip_ahead(step),
            )
            return carry

        lax.fori_loop(1, chips, body, 0)

    adam_piece(r)
    send_piece(r, own_rows, z_send, z_recv)

    drain(comb.at[across_rows], c_recv.at[0])
    adam_piece(across)
    send_piece(across, across_rows, w_send, w_recv)

    def forward_z(step, carry):
        place = params.at[rows(chip_behind(step) * block + r * piece, piece)]
        drain(place, z_recv.at[step])
        return other_reps(lambda j: remote(place, place, f_send, f_recv.at[step], j, f), carry)

    lax.fori_loop(1, chips, forward_z, 0)

    drain(comb.at[pl.ds(0, (reps - 2) * piece)], c_recv.at[1])
    other_reps(adam_piece, 0)
    own_block = params.at[rows(f * block, block)]
    remote(rounded, own_block, s_send, s_recv, r, sibling)
    stores = [pltpu.make_async_copy(rounded, own_block, local_sem.at[3])] + [
        pltpu.make_async_copy(state.at[i], dst, local_sem.at[i])
        for i, dst in enumerate((master_out, first_out, second_out))
    ]
    for store in stores:
        store.start()

    def to_sibling(step, carry):
        start = chip_behind(step) * block
        drain(params.at[rows(start, block - 2 * piece)], f_recv.at[step])
        drain(params.at[rows(start + across * piece, piece)], w_recv.at[step])
        place = params.at[rows(start, block)]
        remote(place, place, s_send, s_recv, r, sibling)
        return carry

    lax.fori_loop(1, chips, to_sibling, 0)
    drain(params.at[pl.ds(0, chips * block)], s_recv)

    for store in stores:
        store.wait()
    drain(x_all.at[pl.ds(0, chips * tokens)], x_send.at[2])

    def drain_x(step, carry):
        @pl.when((chip + 1 < chips) & (chip >= step))
        def _():
            drain(x_slot(chip), x_send.at[0])

        @pl.when((chip > 0) & (chip + step < chips))
        def _():
            drain(x_slot(chip), x_send.at[1])

        return carry

    lax.fori_loop(0, chips - 1, drain_x, 0)

    def drain_y(s, carry):
        drain(y_all.at[s, pl.ds(0, (n - 1) * tokens)], y_send.at[s])
        return carry

    lax.fori_loop(0, chunks, drain_y, 0)
    drain(pieces.at[pl.ds(0, reps - 1)], p_send)
    drain(dots_rep.at[pl.ds(0, reps - 1)], d_send.at[0])
    drain(dots_fsdp.at[pl.ds(0, n - 1)], d_send.at[1])
    drain(comb.at[pl.ds(0, (reps - 1) * piece)], c_send)
    drain(params.at[pl.ds(0, (chips - 1) * piece)], z_send)
    drain(params.at[pl.ds(0, (chips - 1) * piece)], w_send)
    drain(params.at[pl.ds(0, (chips - 1) * (reps - 2) * piece)], f_send)
    drain(params.at[pl.ds(0, chips * block)], s_send)


def hand_out(parts, *refs):
    wide_in, params_in = refs[0:3], refs[3]
    wide_out, params_out = refs[4:7], refs[7]
    wide, narrow, in_sem, out_sem = refs[8:]
    size = params_in.shape[0] // parts
    moves = [(params_in.at[pl.ds(i * size, size)], narrow.at[i], params_out.at[pl.ds(i * size, size)]) for i in range(parts)]
    moves += [(src, wide.at[i], dst) for i, (src, dst) in enumerate(zip(wide_in, wide_out))]
    loads = [pltpu.make_async_copy(src, mid, in_sem.at[i]) for i, (src, mid, _) in enumerate(moves)]
    stores = [pltpu.make_async_copy(mid, dst, out_sem.at[i]) for i, (_, mid, dst) in enumerate(moves)]
    for load in loads:
        load.start()
    for load, store in zip(loads, stores):
        load.wait()
        store.start()
    for store in stores:
        store.wait()


def handed_out(results):
    parts = 8
    wide, params = results[0].shape, results[3].shape
    any_spec = pl.BlockSpec(memory_space=pl.ANY)
    return pl.pallas_call(
        functools.partial(hand_out, parts),
        out_shape=tuple(jax.ShapeDtypeStruct(x.shape, x.dtype) for x in results),
        in_specs=[any_spec] * 4,
        out_specs=[any_spec] * 4,
        scratch_shapes=[
            pltpu.VMEM((3, *wide), jnp.float32),
            pltpu.VMEM((parts, params[0] // parts, params[1]), jnp.bfloat16),
            pltpu.SemaphoreType.DMA((parts + 3,)),
            pltpu.SemaphoreType.DMA((parts + 3,)),
        ],
        compiler_params=pltpu.CompilerParams(vmem_limit_bytes=56 * 2**20),
    )(*results)


def local(reps, n, activations, output_grads, master, first_moment, second_moment):
    tokens, features = activations.shape
    block = master.shape[0]
    chunks = max(1, min(reps, block // 128))
    width = block // chunks
    piece = block // reps
    dot_rows = -(-len(gram_pairs(reps)) // 8) * 8
    wide = jax.ShapeDtypeStruct(master.shape, jnp.float32)
    any_spec = pl.BlockSpec(memory_space=pl.ANY)
    dma = pltpu.SemaphoreType.DMA
    results = pl.pallas_call(
        functools.partial(kernel, reps, n),
        out_shape=(
            wide,
            wide,
            wide,
            jax.ShapeDtypeStruct((n * block, features), jnp.bfloat16),
        ),
        in_specs=[any_spec] * 5,
        out_specs=[any_spec] * 4,
        scratch_shapes=[
            pltpu.VMEM((chunks, n * tokens, width), jnp.bfloat16),
            pltpu.VMEM((n * tokens, features), jnp.bfloat16),
            pltpu.VMEM((block, features), jnp.float32),
            pltpu.VMEM((reps, piece, features), jnp.float32),
            pltpu.VMEM((block, features), jnp.float32),
            pltpu.VMEM((3, block, features), jnp.float32),
            pltpu.VMEM((block, features), jnp.bfloat16),
            pltpu.VMEM((dot_rows, 128), jnp.float32),
            pltpu.VMEM((reps, dot_rows, 128), jnp.float32),
            pltpu.VMEM((dot_rows, 128), jnp.float32),
            pltpu.VMEM((n, dot_rows, 128), jnp.float32),
            dma((4,)),
            dma((chunks,)),
            dma((3,)),
            dma((2, n // 2)),
            dma,
            dma((chunks,)),
            dma((chunks,)),
            dma,
            dma,
            dma((2,)),
            dma((2,)),
            dma,
            dma((2,)),
            dma,
            dma((n // 2,)),
            dma,
            dma((n // 2,)),
            dma,
            dma((n // 2,)),
            dma,
            dma,
        ],
        compiler_params=pltpu.CompilerParams(
            collective_id=0, has_side_effects=True, vmem_limit_bytes=56 * 2**20
        ),
    )(activations, output_grads, master, first_moment, second_moment)
    return handed_out(results)


def solution(mesh):
    in_specs = (
        P(("rep", "fsdp"), None),
        P(("rep", "fsdp"), None),
        P("fsdp", None),
        P("fsdp", None),
        P("fsdp", None),
    )
    out_specs = (P("fsdp", None), P("fsdp", None), P("fsdp", None), P())
    body = functools.partial(local, mesh.shape["rep"], mesh.shape["fsdp"])
    return jax.shard_map(body, mesh=mesh, in_specs=in_specs, out_specs=out_specs, check_vma=False)
```

```python
import functools

import jax
import jax.numpy as jnp
from jax import lax
from jax.experimental import pallas as pl
from jax.experimental.pallas import tpu as pltpu
from jax.sharding import PartitionSpec as P

dot_epsilon = 1e-06
beta_one = 0.9
beta_two = 0.95
adam_epsilon = 1e-08
learn_rate = 0.02
decay_rate = 0.1
correct_one = 1.0 - (beta_one**50) ** 2
correct_two = 1.0 - (beta_two**50) ** 2
contract_first = (((0,), (0,)), ((), ()))
MESH = pl.DeviceIdType.MESH


def drain(ref, sem):
    pltpu.make_async_copy(ref, ref, sem).wait()


def gram_pairs(count):
    return [(i, j) for i in range(count) for j in range(i, count)]


def adasum_coefs(gram, count):
    coefs = [None] * count
    members = [[i] for i in range(count)]
    scale = [1.0] * count

    def inner(left, right):
        total = 0.0
        for i in left:
            for j in right:
                total = total + scale[i] * scale[j] * gram[min(i, j), max(i, j)]
        return total

    while len(members) > 1:
        merged = []
        for left, right in zip(members[::2], members[1::2]):
            cross = inner(left, right)
            left_sq = jnp.maximum(inner(left, left), 0.0)
            right_sq = jnp.maximum(inner(right, right), 0.0)
            left_coef = 1.0 - cross / (2.0 * (left_sq + dot_epsilon))
            right_coef = 1.0 - cross / (2.0 * (right_sq + dot_epsilon))
            for i in left:
                scale[i] = left_coef * scale[i]
            for i in right:
                scale[i] = right_coef * scale[i]
            merged.append(left + right)
        members = merged
    for i in range(count):
        coefs[i] = scale[i]
    return coefs


def kernel(
    reps,
    n,
    act,
    og,
    master_in,
    first_in,
    second_in,
    master_out,
    first_out,
    second_out,
    params,
    y_all,
    x_all,
    grad,
    pieces,
    comb,
    state,
    rounded,
    dots_own,
    dots_rep,
    dots_sum,
    dots_fsdp,
    local_sem,
    own_sem,
    x_send,
    x_chain,
    x_recv,
    y_send,
    y_recv,
    p_send,
    p_recv,
    d_send,
    d_recv,
    c_send,
    c_recv,
    z_send,
    z_recv,
    w_send,
    w_recv,
    f_send,
    f_recv,
    s_send,
    s_recv,
):
    r = lax.axis_index("rep")
    f = lax.axis_index("fsdp")
    core = lax.rem(f, 2)
    chip = lax.div(f, 2)
    chips = n // 2
    sibling = chip * 2 + 1 - core
    tokens = act.shape[0]
    block = master_in.shape[0]
    piece = block // reps
    chunks, width = y_all.shape[0], y_all.shape[2]
    per_chunk = reps // chunks

    def remote(src, dst, send, recv, rep_to, fsdp_to):
        pltpu.make_async_remote_copy(
            src_ref=src,
            dst_ref=dst,
            send_sem=send,
            recv_sem=recv,
            device_id={"rep": rep_to, "fsdp": fsdp_to},
            device_id_type=MESH,
        ).start()

    def rows(start, size):
        return pl.ds(pl.multiple_of(start, 16), size)

    state_loads = [
        pltpu.make_async_copy(src, state.at[i], local_sem.at[i])
        for i, src in enumerate((master_in, first_in, second_in))
    ]
    for load in state_loads:
        load.start()
    own_x = pltpu.make_async_copy(act, x_all.at[rows(f * tokens, tokens)], local_sem.at[3])
    own_x.start()

    def own_y(s):
        column = pl.multiple_of(f * block + s * width, 128)
        return pltpu.make_async_copy(
            og.at[:, pl.ds(column, width)],
            y_all.at[s, rows(f * tokens, tokens)],
            own_sem.at[s],
        )

    for s in range(chunks):
        own_y(s).start()

    barrier = pltpu.get_barrier_semaphore()

    def greet_fsdp(step, carry):
        pl.semaphore_signal(
            barrier, inc=1, device_id={"rep": r, "fsdp": lax.rem(f + step, n)}, device_id_type=MESH
        )
        return carry

    lax.fori_loop(1, n, greet_fsdp, 0)

    def greet_rep(step, carry):
        pl.semaphore_signal(
            barrier, inc=1, device_id={"rep": lax.rem(r + step, reps), "fsdp": f}, device_id_type=MESH
        )
        return carry

    lax.fori_loop(1, reps, greet_rep, 0)
    pl.semaphore_wait(barrier, n + reps - 2)

    def x_slot(at_chip):
        return x_all.at[rows((at_chip * 2 + core) * tokens, tokens)]

    def send_x(src, slot, way, step):
        @pl.when((chip + 1 < chips) if way == 0 else (chip > 0))
        def _():
            to = (chip + 1 - 2 * way) * 2 + core
            remote(src, slot, x_send.at[way], x_chain.at[way, step], r, to)

    for way in range(2):
        send_x(act, x_slot(chip), way, 0)
    remote(act, x_slot(chip), x_send.at[2], x_recv, r, sibling)

    def place_of(s):
        return lax.rem(r + 1 + s, chunks)

    def send_y(index, carry):
        s = place_of(index // (n - 1))
        to = lax.rem(f + 1 + (index + n // 2 - 1) % (n - 1), n)
        column = pl.multiple_of(to * block + s * width, 128)
        remote(
            og.at[:, pl.ds(column, width)],
            y_all.at[s, rows(f * tokens, tokens)],
            y_send.at[s],
            y_recv.at[s],
            r,
            to,
        )
        return carry

    early = (chunks + 1) // 2 * (n - 1)
    lax.fori_loop(0, early, send_y, 0)

    def relay_x(step, carry):
        for way in range(2):
            origin = chip - step * (1 - 2 * way)

            @pl.when((origin >= 0) if way == 0 else (origin < chips))
            def _():
                slot = x_slot(origin)
                drain(slot, x_chain.at[way, step - 1])
                send_x(slot, slot, way, step)
                remote(slot, slot, x_send.at[2], x_recv, r, sibling)

        return carry

    lax.fori_loop(1, chips, relay_x, 0)
    lax.fori_loop(early, chunks * (n - 1), send_y, 0)
    own_x.wait()
    drain(x_all.at[pl.ds(0, chips * tokens)], x_recv)

    depth = min(n * tokens, 2048)

    def chunk_sum(at_chunk, carry):
        s = place_of(at_chunk)
        own_y(s).wait()
        drain(y_all.at[s, pl.ds(0, (n - 1) * tokens)], y_recv.at[s])
        target = rows(s * width, width)
        grad[target, :] = lax.dot_general(
            y_all[s, pl.ds(0, depth), :],
            x_all[pl.ds(0, depth), :],
            contract_first,
            preferred_element_type=jnp.float32,
        )

        def more(at, inner):
            span = rows(at * depth, depth)
            grad[target, :] += lax.dot_general(
                y_all[s, span, :],
                x_all[span, :],
                contract_first,
                preferred_element_type=jnp.float32,
            )
            return inner

        lax.fori_loop(1, n * tokens // depth, more, 0)
        for sub in range(per_chunk):
            j = s * per_chunk + sub

            @pl.when(j != r)
            def _():
                remote(
                    grad.at[rows(j * piece, piece)], pieces.at[r], p_send, p_recv, j, f
                )

        return carry

    lax.fori_loop(0, chunks, chunk_sum, 0)
    pieces[r] = grad[rows(r * piece, piece), :]
    drain(pieces.at[pl.ds(0, reps - 1)], p_recv)

    pairs = gram_pairs(reps)
    lanes = 128

    def slab_dots(at, sums):
        span = pl.ds(pl.multiple_of(at * 8, 8), 8)
        parts = [pieces[i, span, :] for i in range(reps)]
        return tuple(total + parts[i] * parts[j] for total, (i, j) in zip(sums, pairs))

    zero = jnp.zeros((8, pieces.shape[2]), jnp.float32)
    sums = lax.fori_loop(0, piece // 8, slab_dots, (zero,) * len(pairs))
    dots_own[...] = jnp.zeros_like(dots_own)
    for at, total in enumerate(sums):
        line = jnp.sum(total, axis=0, keepdims=True)
        folded = line[:, 0:lanes]
        for start in range(lanes, line.shape[1], lanes):
            folded = folded + line[:, start : start + lanes]
        dots_own[at : at + 1, :] = folded

    def send_dots_rep(step, carry):
        remote(dots_own, dots_rep.at[r], d_send.at[0], d_recv.at[0], lax.rem(r + step, reps), f)
        return carry

    lax.fori_loop(1, reps, send_dots_rep, 0)
    dots_rep[r] = dots_own[...]
    drain(dots_rep.at[pl.ds(0, reps - 1)], d_recv.at[0])
    dots_sum[...] = jnp.sum(dots_rep[...], axis=0)

    def send_dots_fsdp(step, carry):
        remote(dots_sum, dots_fsdp.at[f], d_send.at[1], d_recv.at[1], r, lax.rem(f + step, n))
        return carry

    lax.fori_loop(1, n, send_dots_fsdp, 0)
    dots_fsdp[f] = dots_sum[...]
    drain(dots_fsdp.at[pl.ds(0, n - 1)], d_recv.at[1])
    dots_all = jnp.sum(jnp.sum(dots_fsdp[...], axis=0), axis=1, keepdims=True)
    features = pieces.shape[2]
    gram = {
        pair: jnp.broadcast_to(dots_all[at : at + 1, :], (1, features))
        for at, pair in enumerate(pairs)
    }
    coefs = adasum_coefs(gram, reps)

    own_rows = rows(r * piece, piece)
    for load in state_loads:
        load.wait()

    slab = 16

    def step_rows(start, combined):
        span = rows(start, slab)
        new_first = beta_one * state[1, span, :] + (1.0 - beta_one) * combined
        new_second = beta_two * state[2, span, :] + (1.0 - beta_two) * combined * combined
        update = (
            new_first / correct_one / (jnp.sqrt(new_second / correct_two) + adam_epsilon)
            + decay_rate * state[0, span, :]
        )
        new_master = state[0, span, :] - learn_rate * update
        state[0, span, :] = new_master
        state[1, span, :] = new_first
        state[2, span, :] = new_second
        rounded[span, :] = new_master.astype(jnp.bfloat16)

    def own_step(at, carry):
        span = rows(at * slab, slab)
        combined = coefs[0] * pieces[0, span, :]
        for i in range(1, reps):
            combined = combined + coefs[i] * pieces[i, span, :]
        comb[rows(r * piece + at * slab, slab), :] = combined
        return carry

    lax.fori_loop(0, piece // slab, own_step, 0)

    across = reps - 1 - r
    across_rows = rows(across * piece, piece)

    def other_reps(fn, carry):
        def body(step, inner):
            j = lax.rem(r + step, reps)

            @pl.when(j != across)
            def _():
                fn(j)

            return inner

        return lax.fori_loop(1, reps, body, carry)

    remote(comb.at[own_rows], comb.at[own_rows], c_send, c_recv.at[0], across, f)
    other_reps(
        lambda j: remote(comb.at[own_rows], comb.at[own_rows], c_send, c_recv.at[1], j, f), 0
    )

    def adam_piece(j):
        def body(at, carry):
            start = j * piece + at * slab
            step_rows(start, comb[rows(start, slab), :])
            return carry

        lax.fori_loop(0, piece // slab, body, 0)

    def send_chain(src, dst, send, recv, step):
        for way in range(2):

            @pl.when((chip + 1 < chips) if way == 0 else (chip > 0))
            def _():
                to = (chip + 1 - 2 * way) * 2 + core
                remote(src, dst, send.at[way], recv.at[way, step], r, to)

    def from_each(step, fn):
        for way in range(2):
            origin = chip - step * (1 - 2 * way)

            @pl.when((origin >= 0) if way == 0 else (origin < chips))
            def _():
                fn(way, origin)

    def params_piece(origin, j):
        return params.at[rows((origin * 2 + core) * block + j * piece, piece)]

    def relay(j, send, recv, step, fn):
        def one(way, origin):
            place = params_piece(origin, j)
            drain(place, recv.at[way, step - 1])

            @pl.when((chip + 1 < chips) if way == 0 else (chip > 0))
            def _():
                to = (chip + 1 - 2 * way) * 2 + core
                remote(place, place, send.at[way], recv.at[way, step], r, to)

            fn(way, place)

        from_each(step, one)

    def relay_own(step, carry):
        def to_reps(way, place):
            other_reps(
                lambda j: remote(place, place, f_send, f_recv.at[way, step - 1], j, f), 0
            )

        relay(r, z_send, z_recv, step, to_reps)
        return carry

    def relay_across(step, carry):
        relay(across, w_send, w_recv, step, lambda way, place: None)
        return carry

    adam_piece(r)
    send_chain(rounded.at[own_rows], params_piece(chip, r), z_send, z_recv, 0)
    lax.fori_loop(1, min(2, chips), relay_own, 0)

    drain(comb.at[across_rows], c_recv.at[0])
    adam_piece(across)
    send_chain(rounded.at[across_rows], params_piece(chip, across), w_send, w_recv, 0)
    lax.fori_loop(2, chips, relay_own, 0)
    lax.fori_loop(1, min(2, chips), relay_across, 0)

    drain(comb.at[pl.ds(0, (reps - 2) * piece)], c_recv.at[1])
    other_reps(adam_piece, 0)
    own_block = params.at[rows(f * block, block)]
    remote(rounded, own_block, s_send, s_recv, r, sibling)
    stores = [pltpu.make_async_copy(rounded, own_block, local_sem.at[3])] + [
        pltpu.make_async_copy(state.at[i], dst, local_sem.at[i])
        for i, dst in enumerate((master_out, first_out, second_out))
    ]
    for store in stores:
        store.start()

    lax.fori_loop(2, chips, relay_across, 0)

    def to_sibling(step, carry):
        def one(way, origin):
            place = params.at[rows((origin * 2 + core) * block, block)]
            drain(params.at[pl.ds(0, block - 2 * piece)], f_recv.at[way, step - 1])
            remote(place, place, s_send, s_recv, r, sibling)

        from_each(step, one)
        return carry

    lax.fori_loop(1, chips, to_sibling, 0)
    drain(params.at[pl.ds(0, chips * block)], s_recv)

    for store in stores:
        store.wait()
    drain(x_all.at[pl.ds(0, chips * tokens)], x_send.at[2])

    def drain_chain(step, carry):
        @pl.when((chip + 1 < chips) & (chip >= step))
        def _():
            drain(x_slot(chip), x_send.at[0])
            drain(params.at[pl.ds(0, piece)], z_send.at[0])
            drain(params.at[pl.ds(0, piece)], w_send.at[0])

        @pl.when((chip > 0) & (chip + step < chips))
        def _():
            drain(x_slot(chip), x_send.at[1])
            drain(params.at[pl.ds(0, piece)], z_send.at[1])
            drain(params.at[pl.ds(0, piece)], w_send.at[1])

        return carry

    lax.fori_loop(0, chips - 1, drain_chain, 0)

    def drain_y(s, carry):
        drain(y_all.at[s, pl.ds(0, (n - 1) * tokens)], y_send.at[s])
        return carry

    lax.fori_loop(0, chunks, drain_y, 0)
    drain(pieces.at[pl.ds(0, reps - 1)], p_send)
    drain(dots_rep.at[pl.ds(0, reps - 1)], d_send.at[0])
    drain(dots_fsdp.at[pl.ds(0, n - 1)], d_send.at[1])
    drain(comb.at[pl.ds(0, (reps - 1) * piece)], c_send)
    drain(params.at[pl.ds(0, (chips - 1) * (reps - 2) * piece)], f_send)
    drain(params.at[pl.ds(0, chips * block)], s_send)


def hand_out(parts, *refs):
    wide_in, params_in = refs[0:3], refs[3]
    wide_out, params_out = refs[4:7], refs[7]
    wide, narrow, in_sem, out_sem = refs[8:]
    size = params_in.shape[0] // parts
    moves = [(params_in.at[pl.ds(i * size, size)], narrow.at[i], params_out.at[pl.ds(i * size, size)]) for i in range(parts)]
    moves += [(src, wide.at[i], dst) for i, (src, dst) in enumerate(zip(wide_in, wide_out))]
    loads = [pltpu.make_async_copy(src, mid, in_sem.at[i]) for i, (src, mid, _) in enumerate(moves)]
    stores = [pltpu.make_async_copy(mid, dst, out_sem.at[i]) for i, (_, mid, dst) in enumerate(moves)]
    for load in loads:
        load.start()
    for load, store in zip(loads, stores):
        load.wait()
        store.start()
    for store in stores:
        store.wait()


def handed_out(results):
    parts = 8
    wide, params = results[0].shape, results[3].shape
    any_spec = pl.BlockSpec(memory_space=pl.ANY)
    return pl.pallas_call(
        functools.partial(hand_out, parts),
        out_shape=tuple(jax.ShapeDtypeStruct(x.shape, x.dtype) for x in results),
        in_specs=[any_spec] * 4,
        out_specs=[any_spec] * 4,
        scratch_shapes=[
            pltpu.VMEM((3, *wide), jnp.float32),
            pltpu.VMEM((parts, params[0] // parts, params[1]), jnp.bfloat16),
            pltpu.SemaphoreType.DMA((parts + 3,)),
            pltpu.SemaphoreType.DMA((parts + 3,)),
        ],
        compiler_params=pltpu.CompilerParams(vmem_limit_bytes=56 * 2**20),
    )(*results)


def local(reps, n, activations, output_grads, master, first_moment, second_moment):
    tokens, features = activations.shape
    block = master.shape[0]
    chunks = max(1, min(reps, block // 128))
    width = block // chunks
    piece = block // reps
    dot_rows = -(-len(gram_pairs(reps)) // 8) * 8
    wide = jax.ShapeDtypeStruct(master.shape, jnp.float32)
    any_spec = pl.BlockSpec(memory_space=pl.ANY)
    dma = pltpu.SemaphoreType.DMA
    results = pl.pallas_call(
        functools.partial(kernel, reps, n),
        out_shape=(
            wide,
            wide,
            wide,
            jax.ShapeDtypeStruct((n * block, features), jnp.bfloat16),
        ),
        in_specs=[any_spec] * 5,
        out_specs=[any_spec] * 4,
        scratch_shapes=[
            pltpu.VMEM((chunks, n * tokens, width), jnp.bfloat16),
            pltpu.VMEM((n * tokens, features), jnp.bfloat16),
            pltpu.VMEM((block, features), jnp.float32),
            pltpu.VMEM((reps, piece, features), jnp.float32),
            pltpu.VMEM((block, features), jnp.float32),
            pltpu.VMEM((3, block, features), jnp.float32),
            pltpu.VMEM((block, features), jnp.bfloat16),
            pltpu.VMEM((dot_rows, 128), jnp.float32),
            pltpu.VMEM((reps, dot_rows, 128), jnp.float32),
            pltpu.VMEM((dot_rows, 128), jnp.float32),
            pltpu.VMEM((n, dot_rows, 128), jnp.float32),
            dma((4,)),
            dma((chunks,)),
            dma((3,)),
            dma((2, n // 2)),
            dma,
            dma((chunks,)),
            dma((chunks,)),
            dma,
            dma,
            dma((2,)),
            dma((2,)),
            dma,
            dma((2,)),
            dma((2,)),
            dma((2, n // 2)),
            dma((2,)),
            dma((2, n // 2)),
            dma,
            dma((2, n // 2)),
            dma,
            dma,
        ],
        compiler_params=pltpu.CompilerParams(
            collective_id=0, has_side_effects=True, vmem_limit_bytes=56 * 2**20
        ),
    )(activations, output_grads, master, first_moment, second_moment)
    return handed_out(results)


def solution(mesh):
    in_specs = (
        P(("rep", "fsdp"), None),
        P(("rep", "fsdp"), None),
        P("fsdp", None),
        P("fsdp", None),
        P("fsdp", None),
    )
    out_specs = (P("fsdp", None), P("fsdp", None), P("fsdp", None), P())
    body = functools.partial(local, mesh.shape["rep"], mesh.shape["fsdp"])
    return jax.shard_map(body, mesh=mesh, in_specs=in_specs, out_specs=out_specs, check_vma=False)
```
